256 devices in a mesh: ex: 32 (over z, x_hi, core), blk: 8 (over x_lo, y).
Axes of the slice: x: 4 (x_hi: 2, x_lo: 2; x = x_hi * 2 + x_lo), y: 4, z: 8, core: 2. Of those that a mesh axis runs over, the one named last changes fastest.
Arguments:
- acts: bfloat16 [8, 128, 64, 4096], P('blk', 'ex'), may hold values from -6 to 6
- out_grads: bfloat16 [8, 128, 64, 14336], P('blk', 'ex'), may hold values from -6 to 6
- proj_in: bfloat16 [8, 64, 4096], P('blk'), may hold values from -0.09375 to 0.09375
- proj_out: bfloat16 [8, 64, 14336], P('blk'), may hold values from -0.046875 to 0.046875
- queries: bfloat16 [8, 4096, 4096], P('blk', 'ex'), may hold values from -0.03125 to 0.03125
Outputs:
- scores: float32 [128, 4096], P('blk', 'ex')
The draws below stay inside these ranges and needn't reach their ends.
All inputs are finite; a program needn't handle non-finite values.
Results may differ from the reference program's by a relative error of at most 0.005.
Values may be sent and summed in bfloat16 or wider, within the bound.
A program may use at most 64 MiB of HBM per device.

```python
import jax
import jax.numpy as jnp
from jax import lax

D = 4096
FF = 14336
RANK = 64
TOK = 64
EXAMPLES = 128
QUERIES = 4096
BLOCKS = 8


def shard_levels(key, dims, cuts, low, largest):
    def one(position, shards_of):
        steps = jax.random.uniform(jax.random.fold_in(jax.random.fold_in(key, 6), position), (shards_of,), jnp.float32, low / len(cuts), largest / len(cuts))
        return jnp.repeat(jnp.exp(steps), dims[position] // shards_of).reshape((-1,) + (1,) * (len(dims) - position - 1))

    loudness = one(*cuts[0])
    for cut in cuts[1:]:
        loudness = loudness * one(*cut)
    return loudness


def scatter_about(rng, extent, deviation, most, split=(), held_as=jnp.bfloat16):
    gain = shard_levels(rng, extent, split, -0.22, 0.18) if split else 1.0
    entries = jax.random.normal(rng, extent, jnp.float32) * deviation * gain
    return jnp.minimum(jnp.maximum(entries, -most), most).astype(held_as)


def setup_inputs(seed: int = 0) -> dict:
    key_of = jax.random.split(jax.random.key(seed), 6)
    return {
        "acts": scatter_about(key_of[0], (BLOCKS, EXAMPLES, TOK, D), 1.0, 6.0, ((0, 8), (1, 32))),
        "out_grads": scatter_about(key_of[1], (BLOCKS, EXAMPLES, TOK, FF), 1.0, 6.0, ((0, 8), (1, 32))),
        "proj_in": scatter_about(key_of[2], (BLOCKS, RANK, D), D ** -0.5, 0.09375, ((0, 8),)),
        "proj_out": scatter_about(key_of[3], (BLOCKS, RANK, FF), FF ** -0.5, 0.046875, ((0, 8),)),
        "queries": scatter_about(key_of[4], (BLOCKS, QUERIES, RANK * RANK), (BLOCKS * RANK * RANK) ** -0.5, 0.03125, ((0, 8), (1, 32))),
    }


def block_scores(items):
    acts_b, grads_b, pin_b, pout_b, query_b = items
    rows_in = acts_b.reshape(-1, acts_b.shape[-1])
    rows_out = grads_b.reshape(-1, grads_b.shape[-1])
    in_low = jnp.dot(rows_in, pin_b.T, preferred_element_type=jnp.float32).astype(jnp.bfloat16)
    out_low = jnp.dot(rows_out, pout_b.T, preferred_element_type=jnp.float32).astype(jnp.bfloat16)
    in_low = in_low.reshape(acts_b.shape[0], acts_b.shape[1], -1).astype(jnp.float32)
    out_low = out_low.reshape(acts_b.shape[0], acts_b.shape[1], -1).astype(jnp.float32)
    outer = jnp.einsum("itr,its->irs", in_low, out_low)
    flat = outer.reshape(acts_b.shape[0], -1).astype(jnp.bfloat16)
    return jnp.dot(flat, query_b.T, preferred_element_type=jnp.float32)


def reference(acts, out_grads, proj_in, proj_out, queries):
    partial_all = lax.map(block_scores, (acts, out_grads, proj_in, proj_out, queries))
    return jnp.sum(partial_all, axis=0)
```

```python
import jax
import jax.numpy as jnp
from jax import lax
from jax.experimental import pallas as pl
from jax.experimental.pallas import tpu as pltpu
from jax.sharding import PartitionSpec as P

MESH = pl.DeviceIdType.MESH
NZ = 8
NB = 8
EX = 4
TOK = 64
RANK = 64
J = RANK * RANK // 128
NT = (((1,), (1,)), ((), ()))


def slice_at(k):
    if isinstance(k, int):
        return (k + 1) // 2 if k % 2 else (NZ - k // 2) % NZ
    return jnp.where(lax.rem(k, 2) == 1, (k + 1) // 2, lax.rem(NZ - k // 2, NZ))


def kernel(
    acts, outg, pin, pout, q, out,
    vacts, voutg, vpin, vpout, vq, inf, eo, gbuf, fs, part,
    asem, osem, wsem, zss, zrs, xss, xrs, css, crs, rss, rrs, lsem,
):
    ex, blk = lax.axis_index("ex"), lax.axis_index("blk")
    z, xh, core = ex // 4, lax.rem(ex // 2, 2), lax.rem(ex, 2)

    def at(z_, x_, c_):
        return (z_ * 4 + x_ * 2 + c_, blk)

    x_peer = at(z, 1 - xh, core)
    c_peer = at(z, xh, 1 - core)

    load_pin = pltpu.make_async_copy(pin, vpin, wsem.at[0])
    load_pout = pltpu.make_async_copy(pout, vpout, wsem.at[1])
    load_q = pltpu.make_async_copy(q, vq, wsem.at[2])
    load_acts = pltpu.make_async_copy(acts, vacts, asem)

    def load_outg(i):
        return pltpu.make_async_copy(outg.at[i], voutg.at[i], osem.at[i])

    load_pin.start()
    load_acts.start()
    load_pout.start()
    for i in range(EX):
        load_outg(i).start()
    load_q.start()

    barrier = pltpu.get_barrier_semaphore()
    for d in range(1, NZ):
        pl.semaphore_signal(barrier, inc=1, device_id=at(lax.rem(z + d, NZ), xh, core), device_id_type=MESH)
    pl.semaphore_signal(barrier, inc=1, device_id=x_peer, device_id_type=MESH)
    pl.semaphore_signal(barrier, inc=1, device_id=c_peer, device_id_type=MESH)
    for d in range(1, NB):
        pl.semaphore_signal(barrier, inc=1, device_id=(ex, lax.rem(blk + d, NB)), device_id_type=MESH)

    load_pin.wait()
    load_acts.wait()
    low = lax.dot_general(vpin[...], vacts[...], NT, preferred_element_type=jnp.float32)
    low = low.astype(jnp.bfloat16).astype(jnp.float32)
    for h in range(2):
        inf[:, h, :] = low[:, h * 128:(h + 1) * 128]
    for h in range(2):
        for odd in range(2):
            eo[odd * (RANK // 2):(odd + 1) * (RANK // 2), h * 128:(h + 1) * 128] = (
                inf[pl.ds(odd, RANK // 2, stride=2), h, :].astype(jnp.bfloat16)
            )
    load_pout.wait()
    pl.semaphore_wait(barrier, NZ - 1 + 2 + NB - 1)

    def z_copy(d, i):
        return pltpu.make_async_remote_copy(
            src_ref=gbuf.at[0, core, xh, i],
            dst_ref=gbuf.at[NZ - d, core, xh, i],
            send_sem=zss.at[d, i],
            recv_sem=zrs.at[NZ - d, i],
            device_id=at(lax.rem(z + d, NZ), xh, core),
            device_id_type=MESH,
        )

    def x_copy(dz, x_):
        return pltpu.make_async_remote_copy(
            src_ref=gbuf.at[dz, core, x_],
            dst_ref=gbuf.at[dz, core, x_],
            send_sem=xss.at[dz],
            recv_sem=xrs.at[dz],
            device_id=x_peer,
            device_id_type=MESH,
        )

    def c_copy(dz, c_):
        return pltpu.make_async_remote_copy(
            src_ref=gbuf.at[dz, c_],
            dst_ref=gbuf.at[dz, c_],
            send_sem=css.at[dz],
            recv_sem=crs.at[dz],
            device_id=c_peer,
            device_id_type=MESH,
        )

    lane = lax.broadcasted_iota(jnp.int32, (RANK, EX * TOK), 1)

    @pl.loop(0, EX)
    def _(i):
        load_outg(i).wait()
        low = lax.dot_general(voutg[i], vpout[...], NT, preferred_element_type=jnp.float32)
        low = low.astype(jnp.bfloat16)
        mine = jnp.where(lane // TOK == i, eo[...], jnp.zeros_like(eo))
        g = jnp.dot(mine, jnp.concatenate([low] * EX, axis=0), preferred_element_type=jnp.float32)
        g = jnp.concatenate([g[:J], g[J:]], axis=1)
        gbuf[0, core, xh, i] = g.astype(jnp.bfloat16)
        for d in (4, 3, 5, 2, 6, 1, 7):
            z_copy(d, i).start()

    load_q.wait()

    def r_copy(dz, keeper):
        return pltpu.make_async_remote_copy(
            src_ref=part.at[dz],
            dst_ref=out.at[blk],
            send_sem=rss.at[dz],
            recv_sem=rrs.at[blk],
            device_id=(ex, keeper),
            device_id_type=MESH,
        )

    def l_copy(dz):
        return pltpu.make_async_copy(part.at[dz], out.at[blk], lsem)

    @pl.loop(0, NZ + 2)
    def _(k):
        @pl.when(k < NZ)
        def _():
            dz = slice_at(k)

            @pl.when(k > 0)
            def _():
                for i in range(EX):
                    pltpu.make_async_copy(gbuf.at[dz, core, xh, i], gbuf.at[dz, core, xh, i], zrs.at[dz, i]).wait()

            x_copy(dz, xh).start()

        @pl.when(jnp.logical_and(k >= 1, k < NZ + 1))
        def _():
            dz = slice_at(k - 1)
            x_copy(dz, 1 - xh).wait_recv()
            c_copy(dz, core).start()

        @pl.when(k >= 2)
        def _():
            dz = slice_at(k - 2)
            c_copy(dz, 1 - core).wait_recv()
            for x_ in range(2):
                for c_ in range(2):
                    for i in range(EX):
                        row = (x_ * 2 + c_) * EX + i
                        fs[row * J:(row + 1) * J, :] = gbuf[dz, c_, x_, i].astype(jnp.float32)
            rows = jnp.concatenate(
                [fs[pl.ds(j, 16, stride=J), :].astype(jnp.bfloat16) for j in range(J)], axis=1
            )
            part[dz] = lax.dot_general(rows, vq[...], NT, preferred_element_type=jnp.float32)
            keeper = lax.rem(z + dz, NB)

            @pl.when(keeper == blk)
            def _():
                l_copy(dz).start()

            @pl.when(keeper != blk)
            def _():
                r_copy(dz, keeper).start()

    @pl.loop(0, NZ)
    def _(dz):
        @pl.when(dz > 0)
        def _():
            for i in range(EX):
                z_copy(dz, i).wait_send()

        x_copy(dz, xh).wait_send()
        c_copy(dz, core).wait_send()
        keeper = lax.rem(z + dz, NB)

        @pl.when(keeper == blk)
        def _():
            l_copy(dz).wait()

        @pl.when(keeper != blk)
        def _():
            r_copy(dz, keeper).wait_send()

    @pl.loop(0, NB)
    def _(s):
        @pl.when(s != blk)
        def _():
            pltpu.make_async_copy(out.at[s], out.at[s], rrs.at[s]).wait()


def shards(acts, out_grads, proj_in, proj_out, queries):
    d, ff = acts.shape[3], out_grads.shape[3]
    nq, nk = queries.shape[1:]
    bf16, f32 = jnp.bfloat16, jnp.float32
    dma = pltpu.SemaphoreType.DMA
    terms = pl.pallas_call(
        kernel,
        out_shape=jax.ShapeDtypeStruct((NB, 16, nq), f32),
        in_specs=[pl.BlockSpec(memory_space=pl.ANY)] * 5,
        out_specs=pl.BlockSpec(memory_space=pl.ANY),
        scratch_shapes=[
            pltpu.VMEM((EX * TOK, d), bf16),
            pltpu.VMEM((EX, TOK, ff), bf16),
            pltpu.VMEM((RANK, d), bf16),
            pltpu.VMEM((RANK, ff), bf16),
            pltpu.VMEM((nq, nk), bf16),
            pltpu.VMEM((RANK, 2, 128), f32),
            pltpu.VMEM((RANK, EX * TOK), bf16),
            pltpu.VMEM((NZ, 2, 2, EX, J, 128), bf16),
            pltpu.VMEM((16 * J, 128), f32),
            pltpu.VMEM((NZ, 16, nq), f32),
            dma,
            dma((EX,)),
            dma((3,)),
            dma((NZ, EX)),
            dma((NZ, EX)),
            dma((NZ,)),
            dma((NZ,)),
            dma((NZ,)),
            dma((NZ,)),
            dma((NZ,)),
            dma((NB,)),
            dma,
        ],
        compiler_params=pltpu.CompilerParams(
            collective_id=0, has_side_effects=True, vmem_limit_bytes=60 * 1024 * 1024
        ),
        name="scores",
    )(
        acts.reshape(EX * TOK, d),
        out_grads[0],
        proj_in[0],
        proj_out[0],
        queries[0],
    )
    return jnp.sum(terms, axis=0)


def solution(mesh):
    placed = (
        P("blk", "ex", None, None),
        P("blk", "ex", None, None),
        P("blk", None, None),
        P("blk", None, None),
        P("blk", "ex", None),
    )
    return jax.shard_map(
        shards, mesh=mesh, in_specs=placed, out_specs=P("blk", "ex"), check_vma=False
    )
```

```python
import jax
import jax.numpy as jnp
from jax import lax
from jax.experimental import pallas as pl
from jax.experimental.pallas import tpu as pltpu
from jax.sharding import PartitionSpec as P

MESH = pl.DeviceIdType.MESH
NZ = 8
NB = 8
NEAR = (2, -2, 1, -1)
EX = 4
TOK = 64
RANK = 64
J = RANK * RANK // 128
NT = (((1,), (1,)), ((), ()))


def kernel(
    acts, outg, pin, pout, q, out,
    vacts, voutg, vpin, vpout, vq, inf, eo, gbuf, fs, part,
    asem, osem, wsem, xss, xrs, zss, zrs, dss, drs, fss, frs, hss, hrs, css, crs, rss, rrs, lsem,
):
    ex, blk = lax.axis_index("ex"), lax.axis_index("blk")
    z, xh, core = ex // 4, lax.rem(ex // 2, 2), lax.rem(ex, 2)

    def at(dz, x_, c_):
        return (lax.rem(z + dz + NZ, NZ) * 4 + x_ * 2 + c_, blk)

    x_peer = at(0, 1 - xh, core)
    c_peer = at(0, xh, 1 - core)

    load_pin = pltpu.make_async_copy(pin, vpin, wsem.at[0])
    load_pout = pltpu.make_async_copy(pout, vpout, wsem.at[1])
    load_q = pltpu.make_async_copy(q, vq, wsem.at[2])
    load_acts = pltpu.make_async_copy(acts, vacts, asem)

    def load_outg(i):
        return pltpu.make_async_copy(outg.at[i], voutg.at[i], osem.at[i])

    load_pin.start()
    load_acts.start()
    load_pout.start()
    load_outg(0).start()

    barrier = pltpu.get_barrier_semaphore()
    peers = [x_peer, c_peer]
    peers += [at(dz, x_, core) for dz in NEAR for x_ in range(2)]
    peers += [(ex, lax.rem(blk + d, NB)) for d in range(1, NB)]
    for peer in peers:
        pl.semaphore_signal(barrier, inc=1, device_id=peer, device_id_type=MESH)

    load_pin.wait()
    load_acts.wait()
    load_outg(1).start()
    load_outg(2).start()
    low = lax.dot_general(vpin[...], vacts[...], NT, preferred_element_type=jnp.float32)
    low = low.astype(jnp.bfloat16).astype(jnp.float32)
    for h in range(2):
        inf[:, h, :] = low[:, h * 128:(h + 1) * 128]
    for h in range(2):
        for odd in range(2):
            eo[odd * (RANK // 2):(odd + 1) * (RANK // 2), h * 128:(h + 1) * 128] = (
                inf[pl.ds(odd, RANK // 2, stride=2), h, :].astype(jnp.bfloat16)
            )
    load_pout.wait()
    load_outg(3).start()
    pl.semaphore_wait(barrier, len(peers))

    def remote(src, dst, send_sem, recv_sem, device):
        return pltpu.make_async_remote_copy(
            src_ref=src, dst_ref=dst, send_sem=send_sem, recv_sem=recv_sem,
            device_id=device, device_id_type=MESH,
        )

    def x_copy(i):
        block = gbuf.at[0, core, i, xh]
        return remote(block, block, xss.at[i], xrs.at[i], x_peer)

    def z_copy(d, i):
        there = (NZ - d) % NZ
        return remote(
            gbuf.at[0, core, i, xh], gbuf.at[there, core, i, xh],
            zss.at[there, i], zrs.at[there, i], at(d, xh, core),
        )

    def d_copy(d, i):
        there = (NZ - d) % NZ
        return remote(
            gbuf.at[0, core, i, xh], gbuf.at[there, core, i, xh],
            dss.at[there, i], drs.at[there, i], at(d, 1 - xh, core),
        )

    def f_copy(d, i):
        here, there = (NZ - 2 * d) % NZ, (NZ - 3 * d) % NZ
        return remote(
            gbuf.at[here, core, i], gbuf.at[there, core, i],
            fss.at[there, i], frs.at[there, i], at(d, xh, core),
        )

    def h_copy(d, i):
        here, col = (NZ - 2 * d) % NZ, 0 if d > 0 else 1
        return remote(
            gbuf.at[here, core, i, col], gbuf.at[NZ // 2, core, i, col],
            hss.at[col, i], hrs.at[col, i], at(2 * d, xh, core),
        )

    def c_copy(dz, c_):
        block = gbuf.at[dz, c_]
        return remote(block, block, css.at[dz], crs.at[dz], c_peer)

    def arrived(ref, sem):
        pltpu.make_async_copy(ref, ref, sem).wait()

    lane = lax.broadcasted_iota(jnp.int32, (RANK, EX * TOK), 1)

    @pl.loop(0, EX)
    def _(i):
        load_outg(i).wait()

        @pl.when(i == 0)
        def _():
            load_q.start()

        low = lax.dot_general(voutg[i], vpout[...], NT, preferred_element_type=jnp.float32)
        low = low.astype(jnp.bfloat16)
        mine = jnp.where(lane // TOK == i, eo[...], jnp.zeros_like(eo))
        g = jnp.dot(mine, jnp.concatenate([low] * EX, axis=0), preferred_element_type=jnp.float32)
        g = jnp.concatenate([g[:J], g[J:]], axis=1)
        gbuf[0, core, i, xh] = g.astype(jnp.bfloat16)
        for d in NEAR:
            d_copy(d, i).start()
            z_copy(d, i).start()
        x_copy(i).start()

    @pl.loop(0, EX)
    def _(i):
        for dz, d in ((6, 1), (2, -1)):
            arrived(gbuf.at[dz, core, i, 0], zrs.at[dz, i])
            arrived(gbuf.at[dz, core, i, 0], drs.at[dz, i])
            h_copy(d, i).start()
            f_copy(d, i).start()

    for i in range(EX):
        arrived(gbuf.at[0, core, i, 0], xrs.at[i])
        for dz in (1, 7):
            arrived(gbuf.at[dz, core, i, 0], zrs.at[dz, i])
            arrived(gbuf.at[dz, core, i, 0], drs.at[dz, i])
    for dz in (1, 7, 2, 6, 0):
        c_copy(dz, core).start()
    load_q.wait()

    def r_copy(dz, keeper):
        return remote(part.at[dz], out.at[blk], rss.at[dz], rrs.at[blk], (ex, keeper))

    def l_copy(dz):
        return pltpu.make_async_copy(part.at[dz], out.at[blk], lsem)

    @pl.loop(1, NZ // 2 + 1)
    def _(t):
        pair = (t, jnp.where(t == NZ // 2, 0, NZ - t))
        for n, dz in enumerate(pair):
            c_copy(dz, 1 - core).wait_recv()
            for x_ in range(2):
                for c_ in range(2):
                    for i in range(EX):
                        row = ((n * 2 + x_) * 2 + c_) * EX + i
                        fs[row * J:(row + 1) * J, :] = gbuf[dz, c_, i, x_].astype(jnp.float32)
        rows = jnp.concatenate(
            [fs[pl.ds(j, 32, stride=J), :].astype(jnp.bfloat16) for j in range(J)], axis=1
        )
        scores = lax.dot_general(rows, vq[...], NT, preferred_element_type=jnp.float32)
        for n, dz in enumerate(pair):
            part[dz] = scores[n * 16:(n + 1) * 16]
            keeper = lax.rem(z + dz, NB)

            @pl.when(keeper == blk)
            def _():
                l_copy(dz).start()

            @pl.when(keeper != blk)
            def _():
                r_copy(dz, keeper).start()

        @pl.when(t == 1)
        def _():
            for dz in (3, 5):
                for i in range(EX):
                    arrived(gbuf.at[dz, core, i], frs.at[dz, i])
                c_copy(dz, core).start()

        @pl.when(t == 2)
        def _():
            for i in range(EX):
                for col in range(2):
                    arrived(gbuf.at[4, core, i, col], hrs.at[col, i])
            c_copy(4, core).start()

    @pl.loop(0, EX)
    def _(i):
        for d in NEAR:
            d_copy(d, i).wait_send()
            z_copy(d, i).wait_send()
        x_copy(i).wait_send()
        for d in (1, -1):
            h_copy(d, i).wait_send()
            f_copy(d, i).wait_send()

    @pl.loop(0, NZ)
    def _(dz):
        c_copy(dz, core).wait_send()
        keeper = lax.rem(z + dz, NB)

        @pl.when(keeper == blk)
        def _():
            l_copy(dz).wait()

        @pl.when(keeper != blk)
        def _():
            r_copy(dz, keeper).wait_send()

        @pl.when(dz != blk)
        def _():
            arrived(out.at[dz], rrs.at[dz])


def shards(acts, out_grads, proj_in, proj_out, queries):
    d, ff = acts.shape[3], out_grads.shape[3]
    nq, nk = queries.shape[1:]
    bf16, f32 = jnp.bfloat16, jnp.float32
    dma = pltpu.SemaphoreType.DMA
    terms = pl.pallas_call(
        kernel,
        out_shape=jax.ShapeDtypeStruct((NB, 16, nq), f32),
        in_specs=[pl.BlockSpec(memory_space=pl.ANY)] * 5,
        out_specs=pl.BlockSpec(memory_space=pl.ANY),
        scratch_shapes=[
            pltpu.VMEM((EX * TOK, d), bf16),
            pltpu.VMEM((EX, TOK, ff), bf16),
            pltpu.VMEM((RANK, d), bf16),
            pltpu.VMEM((RANK, ff), bf16),
            pltpu.VMEM((nq, nk), bf16),
            pltpu.VMEM((RANK, 2, 128), f32),
            pltpu.VMEM((RANK, EX * TOK), bf16),
            pltpu.VMEM((NZ, 2, EX, 2, J, 128), bf16),
            pltpu.VMEM((32 * J, 128), f32),
            pltpu.VMEM((NZ, 16, nq), f32),
            dma,
            dma((EX,)),
            dma((3,)),
            dma((EX,)),
            dma((EX,)),
            dma((NZ, EX)),
            dma((NZ, EX)),
            dma((NZ, EX)),
            dma((NZ, EX)),
            dma((NZ, EX)),
            dma((NZ, EX)),
            dma((2, EX)),
            dma((2, EX)),
            dma((NZ,)),
            dma((NZ,)),
            dma((NZ,)),
            dma((NB,)),
            dma,
        ],
        compiler_params=pltpu.CompilerParams(
            collective_id=0, has_side_effects=True, vmem_limit_bytes=60 * 1024 * 1024
        ),
        name="scores",
    )(
        acts.reshape(EX * TOK, d),
        out_grads[0],
        proj_in[0],
        proj_out[0],
        queries[0],
    )
    return jnp.sum(terms, axis=0)


def solution(mesh):
    placed = (
        P("blk", "ex", None, None),
        P("blk", "ex", None, None),
        P("blk", None, None),
        P("blk", None, None),
        P("blk", "ex", None),
    )
    return jax.shard_map(
        shards, mesh=mesh, in_specs=placed, out_specs=P("blk", "ex"), check_vma=False
    )
```

```python
import jax
import jax.numpy as jnp
from jax import lax
from jax.experimental import pallas as pl
from jax.experimental.pallas import tpu as pltpu
from jax.sharding import PartitionSpec as P

MESH = pl.DeviceIdType.MESH
NZ = 8
NB = 8
NEAR = (2, -2, 1, -1)
FAR = (4, 3, -3)
LAST = 3
EX = 4
TOK = 64
RANK = 64
J = RANK * RANK // 128
NT = (((1,), (1,)), ((), ()))


def kernel(
    acts, outg, pin, pout, q, out,
    vacts, voutg, vpin, vpout, vq, vqt, inf, gbuf, fs, part, terms,
    asem, osem, wsem, xss, xrs, zss, zrs, dss, drs, fss, frs, hss, hrs, qss, qrs, rss, rrs,
):
    ex, blk = lax.axis_index("ex"), lax.axis_index("blk")
    z, xh, core = ex // 4, lax.rem(ex // 2, 2), lax.rem(ex, 2)

    def at(dz, x_, c_):
        return (lax.rem(z + dz + NZ, NZ) * 4 + x_ * 2 + c_, blk)

    x_peer = at(0, 1 - xh, core)
    c_peer = at(0, xh, 1 - core)

    load_pin = pltpu.make_async_copy(pin, vpin, wsem.at[0])
    load_pout = pltpu.make_async_copy(pout, vpout, wsem.at[1])
    load_q = pltpu.make_async_copy(q, vq, wsem.at[2])

    def load_acts(i):
        return pltpu.make_async_copy(acts.at[i], vacts.at[i], asem.at[i])

    def load_outg(i):
        return pltpu.make_async_copy(outg.at[i], voutg.at[i], osem.at[i])

    load_pin.start()
    load_acts(0).start()
    load_pout.start()
    load_outg(0).start()

    barrier = pltpu.get_barrier_semaphore()
    peers = [x_peer, c_peer]
    peers += [at(dz, x_, core) for dz in NEAR + FAR for x_ in range(2)]
    peers += [(e, lax.rem(blk + d, NB)) for d in range(1, NB) for e in (ex, c_peer[0])]
    for peer in peers:
        pl.semaphore_signal(barrier, inc=1, device_id=peer, device_id_type=MESH)

    def remote(src, dst, send_sem, recv_sem, device):
        return pltpu.make_async_remote_copy(
            src_ref=src, dst_ref=dst, send_sem=send_sem, recv_sem=recv_sem,
            device_id=device, device_id_type=MESH,
        )

    def x_copy(i):
        block = gbuf.at[0, i, xh]
        return remote(block, block, xss.at[i], xrs.at[i], x_peer)

    def z_copy(d, i):
        there = (NZ - d) % NZ
        return remote(
            gbuf.at[0, i, xh], gbuf.at[there, i, xh],
            zss.at[there, i], zrs.at[there, i], at(d, xh, core),
        )

    def d_copy(d, i):
        there = (NZ - d) % NZ
        return remote(
            gbuf.at[0, i, xh], gbuf.at[there, i, xh],
            dss.at[there, i], drs.at[there, i], at(d, 1 - xh, core),
        )

    def f_copy(d, i):
        here, there = (NZ - 2 * d) % NZ, (NZ - 3 * d) % NZ
        return remote(
            gbuf.at[here, i], gbuf.at[there, i],
            fss.at[there, i], frs.at[there, i], at(d, xh, core),
        )

    def h_copy(d, i):
        here, col = (NZ - 2 * d) % NZ, 0 if d > 0 else 1
        return remote(
            gbuf.at[here, i, col], gbuf.at[NZ // 2, i, col],
            hss.at[col, i], hrs.at[col, i], at(2 * d, xh, core),
        )

    q_copy = remote(vqt.at[core], vqt.at[core], qss, qrs, c_peer)

    def arrived(ref, sem):
        pltpu.make_async_copy(ref, ref, sem).wait()

    def direct(dz, i):
        arrived(gbuf.at[dz, i, 0], zrs.at[dz, i])
        arrived(gbuf.at[dz, i, 0], drs.at[dz, i])

    load_pin.wait()
    load_acts(1).start()
    load_outg(1).start()
    load_acts(0).wait()
    load_pout.wait()

    @pl.loop(0, EX)
    def _(i):
        @pl.when(i > 0)
        def _():
            load_acts(i).wait()

        load_outg(i).wait()

        @pl.when(i < EX - 2)
        def _():
            load_acts(i + 2).start()
            load_outg(i + 2).start()

        @pl.when(i == EX - 2)
        def _():
            load_q.start()

        tall = lax.dot_general(vpin[...], vacts[i], NT, preferred_element_type=jnp.float32)
        inf[:, :TOK] = tall.astype(jnp.bfloat16).astype(jnp.float32)
        low = lax.dot_general(voutg[i], vpout[...], NT, preferred_element_type=jnp.float32)
        split = jnp.concatenate(
            [inf[pl.ds(odd, RANK // 2, stride=2), :][:, :TOK] for odd in range(2)], axis=0
        )
        g = jnp.dot(
            split.astype(jnp.bfloat16), low.astype(jnp.bfloat16), preferred_element_type=jnp.float32
        )
        g = jnp.concatenate([g[:J], g[J:]], axis=1)
        gbuf[0, i, xh] = g.astype(jnp.bfloat16)

        @pl.when(i == 0)
        def _():
            pl.semaphore_wait(barrier, len(peers))

        @pl.when(i >= LAST)
        def _():
            for d in FAR:
                d_copy(d, i).start()
                z_copy(d, i).start()

        for d in NEAR:
            d_copy(d, i).start()
            z_copy(d, i).start()
        x_copy(i).start()

    load_q.wait()

    @pl.loop(0, max(LAST, 2))
    def _(i):
        @pl.when(i < 2)
        def _():
            @pl.loop(0, J // 2)
            def _(j):
                k = pl.multiple_of((i * (J // 2) + j) * 128, 128)
                vqt[core, pl.ds(k, 128), :] = vq[:, pl.ds(k, 128)].T

        @pl.when(i == 1)
        def _():
            q_copy.start()

        @pl.when(i < LAST)
        def _():
            for dz, d in ((6, 1), (2, -1)):
                direct(dz, i)
                h_copy(d, i).start()
                f_copy(d, i).start()

    def r_copy(dz, c_, keeper):
        return remote(
            part.at[dz, c_], terms.at[core, blk], rss.at[dz, c_], rrs.at[core, blk],
            (ex - core + c_, keeper),
        )

    def elsewhere(c_, keeper):
        return jnp.logical_or(keeper != blk, c_ != core)

    @pl.loop(0, NZ // 2 + 1)
    def _(t):
        single = lax.rem(t, NZ // 2) == 0
        pair = (t, jnp.where(single, t, NZ - t))

        @pl.when(t == 0)
        def _():
            for i in range(EX):
                arrived(gbuf.at[0, i, 0], xrs.at[i])
            arrived(vqt.at[0], qrs)

        @pl.when(t == 1)
        def _():
            for i in range(EX):
                direct(1, i)
                direct(7, i)

        @pl.when(t == 2)
        def _():
            for i in range(LAST, EX):
                direct(2, i)
                direct(6, i)

        @pl.when(t == 3)
        def _():
            for dz in (3, 5):
                for i in range(EX):
                    if i < LAST:
                        arrived(gbuf.at[dz, i], frs.at[dz, i])
                    else:
                        direct(dz, i)

        @pl.when(t == 4)
        def _():
            for i in range(EX):
                if i < LAST:
                    for col in range(2):
                        arrived(gbuf.at[4, i, col], hrs.at[col, i])
                else:
                    direct(4, i)

        for n, dz in enumerate(pair):
            for x_ in range(2):
                for i in range(EX):
                    row = (n * 2 + x_) * EX + i
                    fs[row * J:(row + 1) * J, :] = gbuf[dz, i, x_].astype(jnp.float32)
        rows = jnp.concatenate(
            [fs[pl.ds(j, 16, stride=J), :].astype(jnp.bfloat16) for j in range(J)], axis=1
        )
        scores = jnp.dot(
            rows, jnp.concatenate([vqt[0], vqt[1]], axis=1), preferred_element_type=jnp.float32
        )

        def finish(n):
            dz = pair[n]
            keeper = lax.rem(z + dz, NB)
            nq = scores.shape[1] // 2
            for c_ in range(2):
                block = scores[n * 8:(n + 1) * 8, c_ * nq:(c_ + 1) * nq]

                @pl.when(elsewhere(c_, keeper))
                def _():
                    part[dz, c_] = block
                    r_copy(dz, c_, keeper).start()

                @pl.when(jnp.logical_not(elsewhere(c_, keeper)))
                def _():
                    terms[core, blk] = block

        finish(0)

        @pl.when(jnp.logical_not(single))
        def _():
            finish(1)

    q_copy.wait_send()

    @pl.loop(0, EX)
    def _(i):
        for d in NEAR:
            d_copy(d, i).wait_send()
            z_copy(d, i).wait_send()
        x_copy(i).wait_send()

        @pl.when(i < LAST)
        def _():
            for d in (1, -1):
                h_copy(d, i).wait_send()
                f_copy(d, i).wait_send()

        @pl.when(i >= LAST)
        def _():
            for d in FAR:
                d_copy(d, i).wait_send()
                z_copy(d, i).wait_send()

    @pl.loop(0, NZ)
    def _(dz):
        keeper = lax.rem(z + dz, NB)
        for c_ in range(2):
            @pl.when(elsewhere(c_, keeper))
            def _():
                r_copy(dz, c_, keeper).wait_send()

            @pl.when(jnp.logical_or(dz != blk, c_ != core))
            def _():
                arrived(terms.at[c_, dz], rrs.at[c_, dz])

    for c_ in range(2):
        total = jnp.sum(terms[c_], axis=0)
        for x_ in range(2):
            row = (x_ * 2 + c_) * EX
            out[row:row + EX, :] = total[x_ * EX:(x_ + 1) * EX]


def shards(acts, out_grads, proj_in, proj_out, queries):
    d, ff = acts.shape[3], out_grads.shape[3]
    nq, nk = queries.shape[1:]
    bf16, f32 = jnp.bfloat16, jnp.float32
    dma = pltpu.SemaphoreType.DMA
    return pl.pallas_call(
        kernel,
        out_shape=pltpu.VMEM((16, nq), f32),
        in_specs=[pl.BlockSpec(memory_space=pl.ANY)] * 5,
        out_specs=pl.BlockSpec(memory_space=pltpu.VMEM),
        scratch_shapes=[
            pltpu.VMEM((EX, TOK, d), bf16),
            pltpu.VMEM((EX, TOK, ff), bf16),
            pltpu.VMEM((RANK, d), bf16),
            pltpu.VMEM((RANK, ff), bf16),
            pltpu.VMEM((nq, nk), bf16),
            pltpu.VMEM((2, nk, nq), bf16),
            pltpu.VMEM((RANK, 128), f32),
            pltpu.VMEM((NZ, EX, 2, J, 128), bf16),
            pltpu.VMEM((16 * J, 128), f32),
            pltpu.VMEM((NZ, 2, 8, nq), f32),
            pltpu.VMEM((2, NB, 8, nq), f32),
            dma((EX,)),
            dma((EX,)),
            dma((3,)),
            dma((EX,)),
            dma((EX,)),
            dma((NZ, EX)),
            dma((NZ, EX)),
            dma((NZ, EX)),
            dma((NZ, EX)),
            dma((NZ, EX)),
            dma((NZ, EX)),
            dma((2, EX)),
            dma((2, EX)),
            dma,
            dma,
            dma((NZ, 2)),
            dma((2, NB)),
        ],
        compiler_params=pltpu.CompilerParams(
            collective_id=0, has_side_effects=True, vmem_limit_bytes=60 * 1024 * 1024
        ),
        name="scores",
    )(acts[0], out_grads[0], proj_in[0], proj_out[0], queries[0])


def solution(mesh):
    placed = (
        P("blk", "ex", None, None),
        P("blk", "ex", None, None),
        P("blk", None, None),
        P("blk", None, None),
        P("blk", "ex", None),
    )
    return jax.shard_map(
        shards, mesh=mesh, in_specs=placed, out_specs=P("blk", "ex"), check_vma=False
    )
```

```python
import jax
import jax.numpy as jnp
from jax import lax
from jax.experimental import pallas as pl
from jax.experimental.pallas import tpu as pltpu
from jax.sharding import PartitionSpec as P

MESH = pl.DeviceIdType.MESH
NZ = 8
NB = 8
NEAR = (2, -2, 1, -1)
FAR = (4,)
LAST = 3
EX = 4
TOK = 64
RANK = 64
J = RANK * RANK // 128
NT = (((1,), (1,)), ((), ()))


def kernel(
    acts, outg, pin, pout, q, out,
    vacts, voutg, vpin, vpout, vq, inf, gbuf, fs, part, terms,
    asem, osem, wsem, xss, xrs, zss, zrs, dss, drs, fss, frs, hss, hrs, qss, qrs, rss, rrs,
):
    ex, blk = lax.axis_index("ex"), lax.axis_index("blk")
    z, xh, core = ex // 4, lax.rem(ex // 2, 2), lax.rem(ex, 2)

    def at(dz, x_, c_):
        return (lax.rem(z + dz + NZ, NZ) * 4 + x_ * 2 + c_, blk)

    x_peer = at(0, 1 - xh, core)
    c_peer = at(0, xh, 1 - core)

    load_pin = pltpu.make_async_copy(pin, vpin, wsem.at[0])
    load_pout = pltpu.make_async_copy(pout, vpout, wsem.at[1])
    load_q = pltpu.make_async_copy(q, vq.at[core], wsem.at[2])

    def load_acts(i):
        return pltpu.make_async_copy(acts.at[i], vacts.at[i], asem.at[i])

    def load_outg(i):
        return pltpu.make_async_copy(outg.at[i], voutg.at[i], osem.at[i])

    load_pin.start()
    load_acts(0).start()
    load_pout.start()
    load_outg(0).start()

    barrier = pltpu.get_barrier_semaphore()
    peers = [x_peer, c_peer]
    peers += [at(dz, x_, core) for dz in NEAR + FAR for x_ in range(2)]
    peers += [(e, lax.rem(blk + d, NB)) for d in range(1, NB) for e in (ex, c_peer[0])]
    for peer in peers:
        pl.semaphore_signal(barrier, inc=1, device_id=peer, device_id_type=MESH)

    def remote(src, dst, send_sem, recv_sem, device):
        return pltpu.make_async_remote_copy(
            src_ref=src, dst_ref=dst, send_sem=send_sem, recv_sem=recv_sem,
            device_id=device, device_id_type=MESH,
        )

    def x_copy(i):
        block = gbuf.at[0, i, xh]
        return remote(block, block, xss.at[i], xrs.at[i], x_peer)

    def z_copy(d, i):
        there = (NZ - d) % NZ
        return remote(
            gbuf.at[0, i, xh], gbuf.at[there, i, xh],
            zss.at[there, i], zrs.at[there, i], at(d, xh, core),
        )

    def d_copy(d, i):
        there = (NZ - d) % NZ
        return remote(
            gbuf.at[0, i, xh], gbuf.at[there, i, xh],
            dss.at[there, i], drs.at[there, i], at(d, 1 - xh, core),
        )

    def f_copy(d, i):
        here, there = (NZ - 2 * d) % NZ, (NZ - 3 * d) % NZ
        return remote(
            gbuf.at[here, i], gbuf.at[there, i],
            fss.at[there, i], frs.at[there, i], at(d, xh, core),
        )

    def h_copy(d, i):
        here, col = (NZ - 2 * d) % NZ, 0 if d > 0 else 1
        return remote(
            gbuf.at[here, i, col], gbuf.at[NZ // 2, i, col],
            hss.at[col, i], hrs.at[col, i], at(2 * d, xh, core),
        )

    q_copy = remote(q, vq.at[core], qss, qrs, c_peer)

    def arrived(ref, sem):
        pltpu.make_async_copy(ref, ref, sem).wait()

    def direct(dz, i):
        arrived(gbuf.at[dz, i, 0], zrs.at[dz, i])
        arrived(gbuf.at[dz, i, 0], drs.at[dz, i])

    load_pin.wait()
    load_acts(1).start()
    load_outg(1).start()
    load_acts(0).wait()
    load_pout.wait()

    @pl.loop(0, EX)
    def _(i):
        @pl.when(i > 0)
        def _():
            load_acts(i).wait()

        load_outg(i).wait()

        @pl.when(i < EX - 2)
        def _():
            load_acts(i + 2).start()
            load_outg(i + 2).start()

        @pl.when(i == EX - 2)
        def _():
            load_q.start()

        tall = lax.dot_general(vpin[...], vacts[i], NT, preferred_element_type=jnp.float32)
        inf[:, :TOK] = tall.astype(jnp.bfloat16).astype(jnp.float32)
        low = lax.dot_general(voutg[i], vpout[...], NT, preferred_element_type=jnp.float32)
        split = jnp.concatenate(
            [inf[pl.ds(odd, RANK // 2, stride=2), :][:, :TOK] for odd in range(2)], axis=0
        )
        g = jnp.dot(
            split.astype(jnp.bfloat16), low.astype(jnp.bfloat16), preferred_element_type=jnp.float32
        )
        g = jnp.concatenate([g[:J], g[J:]], axis=1)
        gbuf[0, i, xh] = g.astype(jnp.bfloat16)

        @pl.when(i == 0)
        def _():
            pl.semaphore_wait(barrier, len(peers))

        @pl.when(i >= LAST)
        def _():
            for d in FAR:
                d_copy(d, i).start()
                z_copy(d, i).start()

        for d in NEAR:
            d_copy(d, i).start()
            z_copy(d, i).start()
        x_copy(i).start()

        @pl.when(i == 0)
        def _():
            q_copy.start()

    @pl.loop(0, EX)
    def _(i):
        for dz, d in ((6, 1), (2, -1)):
            direct(dz, i)

            @pl.when(i < LAST)
            def _():
                h_copy(d, i).start()

            f_copy(d, i).start()

    load_q.wait()

    def r_copy(dz, c_, keeper):
        return remote(
            part.at[dz, c_], terms.at[core, blk], rss.at[dz, c_], rrs.at[core, blk],
            (ex - core + c_, keeper),
        )

    def elsewhere(c_, keeper):
        return jnp.logical_or(keeper != blk, c_ != core)

    @pl.loop(0, 2)
    def _(t):
        slots = (4 * t, 1 + 2 * t, 7 - 2 * t, 2 + 4 * t)

        @pl.when(t == 0)
        def _():
            for i in range(EX):
                arrived(gbuf.at[0, i, 0], xrs.at[i])
                direct(1, i)
                direct(7, i)
            arrived(vq.at[0], qrs)

        @pl.when(t == 1)
        def _():
            for i in range(EX):
                for dz in (3, 5):
                    arrived(gbuf.at[dz, i], frs.at[dz, i])
                if i < LAST:
                    for col in range(2):
                        arrived(gbuf.at[4, i, col], hrs.at[col, i])
                else:
                    direct(4, i)

        for n, dz in enumerate(slots):
            for x_ in range(2):
                for i in range(EX):
                    row = (n * 2 + x_) * EX + i
                    fs[row * J:(row + 1) * J, :] = gbuf[dz, i, x_].astype(jnp.float32)
        rows = jnp.concatenate(
            [fs[pl.ds(j, 32, stride=J), :].astype(jnp.bfloat16) for j in range(J)], axis=1
        )
        both = jnp.concatenate([vq[0], vq[1]], axis=0)
        scores = lax.dot_general(rows, both, NT, preferred_element_type=jnp.float32)

        def finish(n):
            dz = slots[n]
            keeper = lax.rem(z + dz, NB)
            nq = scores.shape[1] // 2
            for c_ in range(2):
                block = scores[n * 8:(n + 1) * 8, c_ * nq:(c_ + 1) * nq]

                @pl.when(elsewhere(c_, keeper))
                def _():
                    part[dz, c_] = block
                    r_copy(dz, c_, keeper).start()

                @pl.when(jnp.logical_not(elsewhere(c_, keeper)))
                def _():
                    terms[core, blk] = block

        for n in range(len(slots)):
            finish(n)

    q_copy.wait_send()

    @pl.loop(0, EX)
    def _(i):
        for d in NEAR:
            d_copy(d, i).wait_send()
            z_copy(d, i).wait_send()
        x_copy(i).wait_send()

        for d in (1, -1):
            f_copy(d, i).wait_send()

        @pl.when(i < LAST)
        def _():
            for d in (1, -1):
                h_copy(d, i).wait_send()

        @pl.when(i >= LAST)
        def _():
            for d in FAR:
                d_copy(d, i).wait_send()
                z_copy(d, i).wait_send()

    @pl.loop(0, NZ)
    def _(dz):
        keeper = lax.rem(z + dz, NB)
        for c_ in range(2):
            @pl.when(elsewhere(c_, keeper))
            def _():
                r_copy(dz, c_, keeper).wait_send()

            @pl.when(jnp.logical_or(dz != blk, c_ != core))
            def _():
                arrived(terms.at[c_, dz], rrs.at[c_, dz])

    for c_ in range(2):
        total = jnp.sum(terms[c_], axis=0)
        for x_ in range(2):
            row = (x_ * 2 + c_) * EX
            out[row:row + EX, :] = total[x_ * EX:(x_ + 1) * EX]


def shards(acts, out_grads, proj_in, proj_out, queries):
    d, ff = acts.shape[3], out_grads.shape[3]
    nq, nk = queries.shape[1:]
    bf16, f32 = jnp.bfloat16, jnp.float32
    dma = pltpu.SemaphoreType.DMA
    return pl.pallas_call(
        kernel,
        out_shape=pltpu.VMEM((16, nq), f32),
        in_specs=[pl.BlockSpec(memory_space=pl.ANY)] * 5,
        out_specs=pl.BlockSpec(memory_space=pltpu.VMEM),
        scratch_shapes=[
            pltpu.VMEM((EX, TOK, d), bf16),
            pltpu.VMEM((EX, TOK, ff), bf16),
            pltpu.VMEM((RANK, d), bf16),
            pltpu.VMEM((RANK, ff), bf16),
            pltpu.VMEM((2, nq, nk), bf16),
            pltpu.VMEM((RANK, 128), f32),
            pltpu.VMEM((NZ, EX, 2, J, 128), bf16),
            pltpu.VMEM((32 * J, 128), f32),
            pltpu.VMEM((NZ, 2, 8, nq), f32),
            pltpu.VMEM((2, NB, 8, nq), f32),
            dma((EX,)),
            dma((EX,)),
            dma((3,)),
            dma((EX,)),
            dma((EX,)),
            dma((NZ, EX)),
            dma((NZ, EX)),
            dma((NZ, EX)),
            dma((NZ, EX)),
            dma((NZ, EX)),
            dma((NZ, EX)),
            dma((2, EX)),
            dma((2, EX)),
            dma,
            dma,
            dma((NZ, 2)),
            dma((2, NB)),
        ],
        compiler_params=pltpu.CompilerParams(
            collective_id=0, has_side_effects=True, vmem_limit_bytes=60 * 1024 * 1024
        ),
        name="scores",
    )(acts[0], out_grads[0], proj_in[0], proj_out[0], queries[0])


def solution(mesh):
    placed = (
        P("blk", "ex", None, None),
        P("blk", "ex", None, None),
        P("blk", None, None),
        P("blk", None, None),
        P("blk", "ex", None),
    )
    return jax.shard_map(
        shards, mesh=mesh, in_specs=placed, out_specs=P("blk", "ex"), check_vma=False
    )
```
